128 devices in a mesh: krow: 8 (over x, core), tri: 16 (over z, y).
Axes of the slice: x: 4, y: 4, z: 4, core: 2. Of those that a mesh axis runs over, the one named last changes fastest.
Arguments:
- rho_x: bfloat16 [512, 16, 2688], P(('krow', 'tri')), may hold values from -0.83203125 to 0.83203125
- rho_s: bfloat16 [512, 16, 512], P(('krow', 'tri')), may hold values from -1.2578125 to 1.2578125
- coulomb: float32 [2688], replicated, may hold values from 0.1 to 4
- screening: bfloat16 [16, 512, 512], P('tri')
- qmap: int32 [8, 8], replicated, may hold values from 0 to 15, as said below
- qslot: int32 [16], replicated, may hold values from 0 to 15, each once
Outputs:
- kernel: float32 [512, 16, 8192], P(('krow', 'tri'))
The draws below stay inside these ranges and needn't reach their ends.
Inputs may be any that keep to these rules, and one draw needn't show every extreme that they name: qmap is symmetric; qmap[0, 0] is 0 and qmap[0, 8 - 1] is 15; every screening block is symmetric.
All inputs are finite; a program needn't handle non-finite values.
Results may differ from the reference program's by a relative error of at most 0.0032.
Values may be sent and summed in bfloat16 or wider, within the bound.
A program may use at most 128 MiB of HBM per device.

```python
import math
import jax
import jax.numpy as jnp
from jax import lax

NP = 16
NG = 2688
NGW = 512
NK = 512
NQ = 16
N_KROW = 8


def draw_qmap(key, part):
    key = jax.random.fold_in(key, 11)
    base = jax.random.randint(key, (N_KROW, N_KROW), 0, NQ)
    base = base.at[0, 0].set(0).at[0, N_KROW - 1].set(NQ - 1)
    first = lax_iota_rows(N_KROW)
    second = first.T
    return jnp.where(first <= second, base, base.T).astype(jnp.int32)


def lax_iota_rows(count):
    return jnp.broadcast_to(jnp.arange(count, dtype=jnp.int32)[:, None], (count, count))


def draw_screening(key, part):
    key = jax.random.fold_in(key, 23)
    key_off, key_diag = jax.random.split(key, 2)
    noise = jax.random.normal(key_off, (NQ, NGW, NGW), jnp.float32)
    offdiag = (noise + jnp.swapaxes(noise, 1, 2)) * (0.7 * NGW ** (-0.5))
    diag = jax.random.uniform(key_diag, (NQ, NGW), jnp.float32, 1.0, 3.0)
    eye = jnp.eye(NGW, dtype=jnp.float32)
    wmat = offdiag + diag[:, :, None] * eye[None, :, :]
    return wmat.astype(jnp.bfloat16)


def block_levels(stream_key, dims, shards, low, top_value):
    factor_of = 1.0
    for dim, parts in shards:
        steps = jax.random.uniform(jax.random.fold_in(jax.random.fold_in(stream_key, 6), dim), (parts,), jnp.float32, low / len(shards), top_value / len(shards))
        factor_of = factor_of * jnp.repeat(jnp.exp(steps), dims[dim] // parts).reshape((-1,) + (1,) * (len(dims) - 1 - dim))
    return factor_of


def centred(own_key, extent, scale, reach, cuts=(), held_as=jnp.bfloat16):
    array = scale * jax.random.normal(own_key, extent, jnp.float32)
    if cuts:
        array = array * block_levels(own_key, extent, cuts, -0.22, 0.18)
    return jnp.clip(array, -reach, reach).astype(held_as)


def setup_inputs(seed: int = 0) -> dict:
    key_list = jax.random.split(jax.random.key(seed), 7)
    rho_x = centred(key_list[0], (NK, NP, NG), (NG ** -0.25), 0.83203125, ((0, 128),))
    rho_s = centred(key_list[1], (NK, NP, NGW), (NGW ** -0.25), 1.2578125, ((0, 128),))
    coulomb = jnp.clip(jnp.exp(jax.random.uniform(key_list[2], (NG,), jnp.float32, math.log(0.1), math.log(4.0))), 0.1, 4.0)
    screening = draw_screening(jax.random.fold_in(key_list[6], 71), 0)
    qmap = draw_qmap(jax.random.fold_in(key_list[6], 71), 0)
    qslot = jax.random.permutation(key_list[5], NQ).astype(jnp.int32)
    return dict(rho_x=rho_x, rho_s=rho_s, coulomb=coulomb, screening=screening, qmap=qmap, qslot=qslot)


def reference(rho_x, rho_s, coulomb, screening, qmap, qslot):
    scaled = (rho_x.astype(jnp.float32) * jnp.sqrt(coulomb)[None, None, :]).astype(jnp.bfloat16)
    flat = scaled.reshape(NK * NP, NG)
    exch = jnp.dot(flat, flat.T, preferred_element_type=jnp.float32)
    span = NK // N_KROW * NP
    screened = rho_s.reshape(NK * NP, NGW)
    row_blocks = []
    for group in range(N_KROW):
        left = screened[group * span:(group + 1) * span].astype(jnp.float32)
        blocks = []
        for other in range(N_KROW):
            right = screened[other * span:(other + 1) * span]
            wmat = screening[qslot[qmap[group, other]]]
            proj = jnp.dot(wmat, right.T, preferred_element_type=jnp.float32)
            blocks.append(jnp.dot(left, proj, precision=lax.Precision.HIGHEST))
        row_blocks.append(jnp.concatenate(blocks, axis=1))
    direct = jnp.concatenate(row_blocks, axis=0)
    return (2.0 * exch - direct).reshape(NK, NP, NK * NP)
```

```python
import functools

import jax
import jax.numpy as jnp
from jax import lax
from jax.experimental import pallas as pl
from jax.experimental.pallas import tpu as pltpu
from jax.sharding import PartitionSpec as P

MESH = pl.DeviceIdType.MESH
SIDE = 4
CORES = 2
GROUPS = SIDE * CORES
PLANE = SIDE * SIDE

ROWS = ((0, 0), (0, 2), (0, 1), (1, 0), (1, 1), (1, 3), (2, 0), (2, 2), (3, 2), (2, 3))
PAIRS = (2, 4, 8)
EARLY = 6
ROW_FROM = {
    (0, 1): (0, 1), (0, 2): (0, 1), (1, 0): (1, 0), (2, 0): (1, 0), (1, 3): (0, 3),
    (3, 2): (3, 0), (2, 2): (3, 0), (2, 3): (0, 3),
}
W_FROM = {
    (0, 3): (0, 3), (0, 2): (0, 3), (0, 1): (0, 1),
    (3, 0): (3, 0), (3, 1): (3, 0), (3, 2): (3, 0), (3, 3): (3, 0),
    (1, 0): (1, 0), (1, 1): (0, 1), (1, 3): (0, 3), (1, 2): (0, 3),
    (2, 0): (3, 0), (2, 3): (0, 3), (2, 2): (3, 0), (2, 1): (1, 0),
}


def row_from(b, k):
    if b == (1, 1):
        return (1, 0) if k < 2 else (0, 1)
    return ROW_FROM[b]


def less(b, e):
    return ((b[0] - e[0]) % SIDE, (b[1] - e[1]) % SIDE)


def depth(b, source):
    return 0 if b == (0, 0) else 1 + depth(less(b, source(b)), source)


def kernel(parts, rx, rs, cou, w, qmap, qslot, out,
           srow, xrow, scol, xcol, wst, pt, ysend, y, rout, tout, tin, inb, acc, ssem, rsem):
    nb, width = rs.shape
    chunk = xrow.shape[2]
    kr = lax.axis_index("krow")
    tr = lax.axis_index("tri")
    px, pc = kr // CORES, kr % CORES
    pz, py = tr // SIDE, tr % SIDE

    def plane_at(b):
        return ((pz + b[1]) % SIDE) * SIDE + (py + b[0]) % SIDE

    def line_at(dx, dc):
        return ((px + dx) % SIDE) * CORES + (pc + dc) % CORES

    def block(index):
        return pl.ds(pl.multiple_of(index * nb, nb), nb)

    def row(k, slot):
        rows = pl.ds(slot * nb, nb)
        return srow.at[rows] if k == 0 else xrow.at[k - 1, rows]

    def col(k, o):
        return scol.at[block(o)] if k == 0 else xcol.at[k - 1, block(o)]

    line = [(dx, dc) for dx in range(SIDE) for dc in range(CORES) if (dx, dc) != (0, 0)]
    others = [(dy, dz) for dy in range(SIDE) for dz in range(SIDE) if (dy, dz) != (0, 0)]

    barrier = pltpu.get_barrier_semaphore()
    for b in others:
        pl.semaphore_signal(barrier, inc=1, device_id={"tri": plane_at(b)}, device_id_type=MESH)
    for dx, dc in line:
        pl.semaphore_signal(barrier, inc=1, device_id={"krow": line_at(dx, dc)}, device_id_type=MESH)

    wst[tr] = w[block(kr), :]
    srow[0:nb, :] = rs[...]
    scol[block(kr), :] = rs[...]

    def scale(k):
        lanes = pl.ds((k - 1) * chunk, chunk)
        own = (rx[:, lanes].astype(jnp.float32) * jnp.sqrt(cou[:, lanes])).astype(jnp.bfloat16)
        xrow[k - 1, 0:nb, :] = own
        xcol[k - 1, block(kr), :] = own

    scale(1)
    pl.semaphore_wait(barrier, len(others) + len(line))

    copies = {}

    def send(name, src, dst, device):
        i = len(copies)
        copies[name] = pltpu.make_async_remote_copy(
            src_ref=src, dst_ref=dst, send_sem=ssem.at[i], recv_sem=rsem.at[i],
            device_id=device, device_id_type=MESH,
        )
        copies[name].start()

    def send_w(parent):
        for b, e in W_FROM.items():
            if less(b, e) == parent:
                held = wst.at[plane_at(parent)]
                send(("w", b), held, held, {"tri": plane_at((-e[0], -e[1]))})

    def send_row(parent, k):
        for slot, b in enumerate(ROWS):
            if slot and less(b, row_from(b, k)) == parent:
                e = row_from(b, k)
                send(("row", b, k), row(k, ROWS.index(parent)), row(k, slot), {"tri": plane_at((-e[0], -e[1]))})

    def send_col(k):
        for dx in (1, 3, 2):
            send(("col", dx, k), col(k, kr), col(k, kr), {"krow": line_at(-dx, 0)})
        send_sib(0, k)

    def send_sib(dx, k):
        held = col(k, line_at(dx, 0))
        send(("sib", dx, k), held, held, {"krow": line_at(0, 1)})

    def project():
        pt[...] = (
            lax.dot_general(
                wst[...].reshape(PLANE * nb, width), scol[...], (((1,), (1,)), ((), ())),
                preferred_element_type=jnp.float32,
            ) * -0.5
        ).astype(jnp.bfloat16).reshape(pt.shape)
        low = lax.broadcasted_iota(jnp.int32, (nb, 2 * nb), 1) < nb
        for dx, dc in line + [(0, 0)]:
            o = line_at(dx, dc)
            for q in range(GROUPS // 2):
                lanes = pl.ds(q * 2 * nb, 2 * nb)
                first = pt[qslot[qmap[o, 2 * q]], :, lanes]
                second = pt[qslot[qmap[o, 2 * q + 1]], :, lanes]
                ysend[o, :, lanes] = jnp.where(low, first, second)
            if (dx, dc) == (0, 0):
                y[block(kr), :] = ysend[kr]
            else:
                send(("y", dx, dc), ysend.at[o], y.at[block(kr)], {"krow": o})

    def rows_of(group):
        return slice(0, EARLY * nb) if group == 0 else slice(EARLY * nb, len(ROWS) * nb)

    def exchange(group, k):
        rows = rows_of(group)
        part = lax.dot_general(
            xrow[k - 1, rows, :], xcol[k - 1], (((1,), (1,)), ((), ())), preferred_element_type=jnp.float32
        )
        acc[rows, :] = part if k == 1 else acc[rows, :] + part

    def finish(group):
        rows = rows_of(group)
        total = acc[rows, :] + jnp.dot(srow[rows, :], y[...], preferred_element_type=jnp.float32)
        acc[rows, :] = total * 2.0
        rout[rows, :] = acc[rows, :].astype(jnp.bfloat16)
        for slot in range(0, EARLY) if group == 0 else range(EARLY, len(ROWS)):
            if slot == 0:
                inb[tr] = rout[0:nb, :]
            else:
                b = ROWS[slot]
                send(("out", b), rout.at[pl.ds(slot * nb, nb)], inb.at[tr], {"tri": plane_at(b)})
        pairs = [i for i, p in enumerate(PAIRS) if (p < EARLY) == (group == 0)]
        for i in pairs:
            p = PAIRS[i]
            tout[i] = acc[p * nb : (p + 2) * nb, :].T.astype(jnp.bfloat16)
            tin[i, block(kr), :] = tout[i, block(kr), :]
            for dx, dc in line:
                o = line_at(dx, dc)
                send(("flip", i, dx, dc), tout.at[i, block(o)], tin.at[i, block(kr)], {"krow": o})

    events = []
    for b in W_FROM:
        events.append((2.0 * depth(b, W_FROM.get), ("w", b)))
    for k in range(parts + 1):
        for b in ROWS[1:]:
            events.append((3.0 + 2.5 * k + 4.0 * depth(b, lambda v: row_from(v, k)), ("row", b, k)))
        for dx in (1, 3, 2):
            events.append((3.5 + 4.5 * k + (0.5 if dx == 2 else 0), ("col", dx, k)))
        for dx in range(SIDE):
            events.append((5.5 + 4.5 * k, ("sib", dx, k)))
    for dx, dc in line:
        events.append((15.0, ("y", dx, dc)))
    events.sort(key=lambda v: v[0])

    def names(kind, k=None):
        return [name for _, name in events if name[0] == kind and (k is None or name[-1] == k)]

    def group_rows(group, k):
        return [n for n in names("row", k) if (ROWS.index(n[1]) < EARLY) == (group == 0)]

    tasks = [(names("w") + names("col", 0) + names("sib", 0), project)]
    for k in range(1, parts + 1):
        for group in range(2):
            tasks.append(
                (group_rows(group, k) + names("col", k) + names("sib", k), functools.partial(exchange, group, k))
            )
    for group in range(2):
        deps = names("y")
        for k in range(parts + 1):
            deps = deps + group_rows(group, k) + names("col", k) + names("sib", k)
        tasks.append((deps, functools.partial(finish, group)))

    send_w((0, 0))
    send_col(0)
    send_row((0, 0), 0)
    for k in range(1, parts + 1):
        if k > 1:
            scale(k)
        send_col(k)
        send_row((0, 0), k)

    seen = set()
    for _, name in events:
        copies[name].wait_recv()
        seen.add(name)
        if name[0] == "w":
            send_w(name[1])
        elif name[0] == "row":
            send_row(name[1], name[2])
        elif name[0] == "col":
            send_sib(name[1], name[2])
        for task in [t for t in tasks if seen.issuperset(t[0])]:
            task[1]()
            tasks.remove(task)

    low = lax.broadcasted_iota(jnp.int32, (nb, 2 * nb), 1) < nb

    def mix(first, second):
        return (
            jnp.where(low, first, pltpu.roll(second, nb, 1)),
            jnp.where(low, pltpu.roll(first, nb, 1), second),
        )

    for i, p in enumerate(PAIRS):
        for dx, dc in line:
            copies["flip", i, dx, dc].wait_recv()
        for q in range(GROUPS // 2):
            first = tin[i, 2 * q * nb : (2 * q + 1) * nb, :].astype(jnp.float32)
            second = tin[i, (2 * q + 1) * nb : (2 * q + 2) * nb, :].astype(jnp.float32)
            for slot, got in zip((p, p + 1), mix(first, second)):
                inb[plane_at(ROWS[slot]), :, q * 2 * nb : (q + 1) * 2 * nb] = got.astype(jnp.bfloat16)
    for b in ROWS[1:]:
        copies["out", b].wait_recv()
    span = PLANE * nb
    for m in range(PLANE // 2):
        for q in range(GROUPS // 2):
            lanes = slice(q * 2 * nb, (q + 1) * 2 * nb)
            first = inb[2 * m, :, lanes].astype(jnp.float32)
            second = inb[2 * m + 1, :, lanes].astype(jnp.float32)
            for o, got in zip((2 * q, 2 * q + 1), mix(first, second)):
                at = o * span + m * 2 * nb
                out[:, at : at + 2 * nb] = got
    for copy in copies.values():
        copy.wait_send()


def body(rho_x, rho_s, coulomb, screening, qmap, qslot):
    kpoints, npair, waves = rho_x.shape
    width = rho_s.shape[-1]
    nb = kpoints * npair
    parts = 3
    chunk = waves // parts
    cols = GROUPS * nb
    bf16, f32 = jnp.bfloat16, jnp.float32
    vmem = pl.BlockSpec(memory_space=pltpu.VMEM)
    smem = pl.BlockSpec(memory_space=pltpu.SMEM)
    ncopies = 15 + 9 * (parts + 1) + 7 * (parts + 1) + 7 + 9 + 21
    out = pl.pallas_call(
        functools.partial(kernel, parts),
        out_shape=jax.ShapeDtypeStruct((nb, GROUPS * PLANE * nb), f32),
        in_specs=[vmem, vmem, vmem, vmem, smem, smem],
        out_specs=vmem,
        scratch_shapes=[
            pltpu.VMEM((len(ROWS) * nb, width), bf16),
            pltpu.VMEM((parts, len(ROWS) * nb, chunk), bf16),
            pltpu.VMEM((cols, width), bf16),
            pltpu.VMEM((parts, cols, chunk), bf16),
            pltpu.VMEM((PLANE, nb, width), bf16),
            pltpu.VMEM((PLANE, nb, cols), bf16),
            pltpu.VMEM((GROUPS, nb, cols), bf16),
            pltpu.VMEM((width, cols), bf16),
            pltpu.VMEM((len(ROWS) * nb, cols), bf16),
            pltpu.VMEM((len(PAIRS), cols, 2 * nb), bf16),
            pltpu.VMEM((len(PAIRS), cols, 2 * nb), bf16),
            pltpu.VMEM((PLANE, nb, cols), bf16),
            pltpu.VMEM((len(ROWS) * nb, cols), f32),
            pltpu.SemaphoreType.DMA((ncopies,)),
            pltpu.SemaphoreType.DMA((ncopies,)),
        ],
        compiler_params=pltpu.CompilerParams(
            collective_id=0, has_side_effects=True, vmem_limit_bytes=48 * 2**20
        ),
        name="kernel_rows",
    )(
        rho_x.reshape(nb, waves),
        rho_s.reshape(nb, width),
        coulomb.reshape(1, waves),
        screening.reshape(width, width),
        qmap,
        qslot,
    )
    return out.reshape(kpoints, npair, -1)


def solution(mesh):
    placed = (
        P(("krow", "tri"), None, None),
        P(("krow", "tri"), None, None),
        P(),
        P("tri", None, None),
        P(),
        P(),
    )
    return jax.shard_map(
        body, mesh=mesh, in_specs=placed, out_specs=P(("krow", "tri"), None, None), check_vma=False
    )
```

```python
import functools

import jax
import jax.numpy as jnp
from jax import lax
from jax.experimental import pallas as pl
from jax.experimental.pallas import tpu as pltpu
from jax.sharding import PartitionSpec as P

MESH = pl.DeviceIdType.MESH
SIDE = 4
CORES = 2
GROUPS = SIDE * CORES
PLANE = SIDE * SIDE

ROWS = ((0, 0), (2, 0), (3, 0), (0, 3), (1, 3), (0, 2), (2, 1), (1, 2), (2, 2), (1, 1))
PLAN = {
    (0, 1): (
        (0, 1, -1), (0, 2, -1), (1, 1, -1), (2, 1, -1), (3, 2, -1), (1, 2, -1), (2, 2, -1), (3, 3, -1),
        (2, 1, 0), (2, 1, 1), (2, 2, 0), (2, 1, 3), (2, 1, 2), (2, 2, 3),
    ),
    (1, 0): (
        (1, 0, -1), (2, 0, -1), (1, 3, -1), (1, 3, 2), (1, 3, 1), (2, 3, -1), (1, 2, 2), (1, 2, 1),
        (1, 3, 3), (1, 3, 0), (2, 2, 1), (2, 2, 2),
    ),
    (0, 3): (
        (0, 3, -1), (0, 3, 2), (0, 3, 1), (0, 2, 2), (0, 2, 1), (3, 0, -1), (0, 3, 3), (0, 3, 0),
        (1, 1, 2), (0, 2, 3), (0, 2, 0), (1, 2, 3),
    ),
    (3, 0): (
        (3, 0, 1), (3, 0, 0), (3, 1, -1), (2, 0, 1), (2, 0, 0), (3, 0, 3), (3, 0, 2), (2, 0, 3),
        (2, 0, 2), (1, 1, 0), (1, 1, 1), (1, 2, 0), (1, 1, 3),
    ),
}
OUT = tuple(i for i, b in enumerate(ROWS) if i == 1 or b[0] % 2 or b[1] % 2)
FLIP = (2, 4, 6, 8)
PARTS = 3
RATE = 9e4
LATENCY = 1.9
WINDOW = 4


def less(b, e):
    return ((b[0] - e[0]) % SIDE, (b[1] - e[1]) % SIDE)


def transfers(parts, cost):
    links = {}
    for e, entries in PLAN.items():
        links[e] = []
        for dy, dz, k in entries:
            kind, rest = ("w", ()) if k < 0 else ("row", (k,))
            parent = (kind, less((dy, dz), e)) + rest
            need = [parent] if parent[1] != (0, 0) else []
            links[e].append(((kind, (dy, dz)) + rest, cost[0] if k < 0 else cost[k], need))
    for dx in (1, 3):
        order = []
        for k in range(parts + 1):
            order.append((("col", dx, k), cost[k], []))
            if k:
                order.append((("far", dx, k - 1), cost[k - 1] / 2, [("col", dx, k - 1)]))
        links[dx] = order + [(("far", dx, parts), cost[parts] / 2, [("col", dx, parts)])]
    links["sib"] = []
    for k in range(parts + 1):
        for dx in (0, 1, 3, 2):
            need = {0: [], 1: [("col", 1, k)], 3: [("col", 3, k)], 2: [("far", 1, k), ("far", 3, k)]}[dx]
            links["sib"].append((("sib", dx, k), cost[k] / 6, need))
    early = [n for v in links.values() for n, _, _ in v if n[0] == "w" or n[0] in ("col", "far", "sib") and n[-1] == 0]
    links["y"] = [(("y",), 6.0, early)]
    return links


def schedule(links):
    arrive, at, free, steps = {}, dict.fromkeys(links, 0), dict.fromkeys(links, 0.0), []
    while any(at[link] < len(links[link]) for link in links):
        for link, order in links.items():
            while at[link] < len(order) and all(n in arrive for n in order[at[link]][2]):
                name, cost, need = order[at[link]]
                ready = max([arrive[n] for n in need], default=0.0)
                paced = arrive[order[at[link] - WINDOW][0]] if at[link] >= WINDOW else 0.0
                free[link] = max(free[link], ready) + cost
                arrive[name] = free[link] + LATENCY
                steps += [(max(ready, paced), 1, name), (arrive[name], 0, name)]
                at[link] += 1
    return sorted(steps, key=lambda v: v[:2])


def kernel(parts, rx_hbm, rs_hbm, cou_hbm, w_hbm, qmap_hbm, qslot_hbm, out,
           rx, cou, qmap, qslot, srow, xrow, scol, xcol, wst, pt, ysend, y, rout, tout, tin, inb, acc,
           lsem, ssem, rsem):
    width = srow.shape[1]
    nb = rx.shape[0]
    chunk = xrow.shape[2]
    kr = lax.axis_index("krow")
    tr = lax.axis_index("tri")
    px, pc = kr // CORES, kr % CORES
    pz, py = tr // SIDE, tr % SIDE

    def plane_at(b):
        return ((pz + b[1]) % SIDE) * SIDE + (py + b[0]) % SIDE

    def line_at(dx, dc):
        return ((px + dx) % SIDE) * CORES + (pc + dc) % CORES

    def block(index):
        return pl.ds(pl.multiple_of(index * nb, nb), nb)

    def row(k, slot):
        rows = pl.ds(slot * nb, nb)
        return srow.at[rows] if k == 0 else xrow.at[k - 1, rows]

    def col(k, o):
        return scol.at[block(o)] if k == 0 else xcol.at[k - 1, block(o)]

    line = [(dx, dc) for dx in range(SIDE) for dc in range(CORES) if (dx, dc) != (0, 0)]
    others = [(dy, dz) for dy in range(SIDE) for dz in range(SIDE) if (dy, dz) != (0, 0)]

    barrier = pltpu.get_barrier_semaphore()
    for b in others:
        pl.semaphore_signal(barrier, inc=1, device_id={"tri": plane_at(b)}, device_id_type=MESH)
    for dx, dc in line:
        pl.semaphore_signal(barrier, inc=1, device_id={"krow": line_at(dx, dc)}, device_id_type=MESH)

    loads = [
        pltpu.make_async_copy(src, dst, lsem.at[i])
        for i, (src, dst) in enumerate((
            (rx_hbm, rx), (cou_hbm, cou), (rs_hbm, srow.at[0:nb]), (rs_hbm, scol.at[block(kr)]),
            (w_hbm.at[block(kr)], wst.at[tr]), (qmap_hbm, qmap), (qslot_hbm, qslot),
        ))
    ]
    for load in loads:
        load.start()

    def scale(k):
        lanes = pl.ds((k - 1) * chunk, chunk)
        own = (rx[:, lanes].astype(jnp.float32) * jnp.sqrt(cou[lanes]).reshape(1, chunk)).astype(jnp.bfloat16)
        xrow[k - 1, 0:nb, :] = own
        xcol[k - 1, block(kr), :] = own

    out[...] = jnp.zeros_like(out)
    for load in loads:
        load.wait()
    pl.semaphore_wait(barrier, len(others) + len(line))

    copies = {}

    def send(name, src, dst, device):
        i = len(copies)
        copies[name] = pltpu.make_async_remote_copy(
            src_ref=src, dst_ref=dst, send_sem=ssem.at[i], recv_sem=rsem.at[i],
            device_id=device, device_id_type=MESH,
        )
        copies[name].start()

    scaled = set()

    def pass_on(name):
        kind = name[0]
        if kind in ("row", "col") and name[-1] not in scaled | {0}:
            scaled.add(name[-1])
            scale(name[-1])
        if kind == "w":
            b, e = name[1], source[name]
            held = wst.at[plane_at(less(b, e))]
            send(name, held, held, {"tri": plane_at((-e[0], -e[1]))})
        elif kind == "row":
            b, k = name[1:]
            e = source[name]
            send(name, row(k, ROWS.index(less(b, e))), row(k, ROWS.index(b)), {"tri": plane_at((-e[0], -e[1]))})
        elif kind == "col":
            dx, k = name[1:]
            send(name, col(k, kr), col(k, kr), {"krow": line_at(-dx, 0)})
        elif kind == "far":
            dx, k = name[1:]
            held = col(k, line_at(dx, 0)).at[pl.ds(0 if dx == 1 else nb // 2, nb // 2)]
            send(name, held, held, {"krow": line_at(-dx, 0)})
        elif kind == "sib":
            dx, k = name[1:]
            held = col(k, line_at(dx, 0))
            send(name, held, held, {"krow": line_at(0, 1)})
        else:
            project()

    def project():
        pt[...] = (
            lax.dot_general(
                wst[...].reshape(PLANE * nb, width), scol[...], (((1,), (1,)), ((), ())),
                preferred_element_type=jnp.float32,
            ) * -0.5
        ).astype(jnp.bfloat16).reshape(pt.shape)
        low = lax.broadcasted_iota(jnp.int32, (nb, 2 * nb), 1) < nb
        for dx, dc in line + [(0, 0)]:
            o = line_at(dx, dc)
            for q in range(GROUPS // 2):
                lanes = pl.ds(q * 2 * nb, 2 * nb)
                first = pt[qslot[qmap[o, 2 * q]], :, lanes]
                second = pt[qslot[qmap[o, 2 * q + 1]], :, lanes]
                ysend[o, :, lanes] = jnp.where(low, first, second)
            if (dx, dc) == (0, 0):
                y[block(kr), :] = ysend[kr]
            else:
                send(("y", dx, dc), ysend.at[o], y.at[block(kr)], {"krow": o})

    def rows_of(group):
        return slice(group * 2 * nb, (group + 1) * 2 * nb)

    def work(group, k):
        rows = rows_of(group)
        if k == 0:
            part = jnp.dot(srow[rows, :], y[...], preferred_element_type=jnp.float32)
        else:
            part = lax.dot_general(
                xrow[k - 1, rows, :], xcol[k - 1], (((1,), (1,)), ((), ())), preferred_element_type=jnp.float32
            )
        total = part if not done[group] else acc[rows, :] + part
        done[group] += 1
        if done[group] <= parts:
            acc[rows, :] = total
        else:
            finish(group, total)

    def finish(group, total):
        rows = rows_of(group)
        total = total * 2.0
        rout[rows, :] = total.astype(jnp.bfloat16)
        for slot in (2 * group, 2 * group + 1):
            b = ROWS[slot]
            if slot in OUT:
                send(("out", b), rout.at[pl.ds(slot * nb, nb)], inb.at[slot], {"tri": plane_at(b)})
        if 2 * group in FLIP:
            i = FLIP.index(2 * group)
            tout[i] = total.T.astype(jnp.bfloat16)
            for dx, dc in line:
                o = line_at(dx, dc)
                send(("flip", i, dx, dc), tout.at[i, block(o)], tin.at[i, block(kr)], {"krow": o})
            tin[i, block(kr), :] = tout[i, block(kr), :]
        sent.append(group)

    upper = lax.broadcasted_iota(jnp.int32, (nb, 2 * nb), 1) // nb
    span = PLANE * nb

    def place(t, o, half, got, turned):
        lanes = pl.ds(pl.multiple_of(o * span + (t // 2) * 2 * nb, 2 * nb), 2 * nb)
        value = jnp.where(t % 2 == half, got, turned)
        out[:, lanes] = jnp.where(upper == t % 2, value, out[:, lanes].astype(jnp.float32)).astype(out.dtype)

    def gather(group):
        for slot in (2 * group, 2 * group + 1):
            if slot in OUT or slot == 0:
                b = ROWS[slot]
                if slot:
                    copies["out", b].wait_recv()
                held = inb.at[slot] if slot else rout.at[0:nb]
                for q in range(GROUPS // 2):
                    got = held[:, q * 2 * nb : (q + 1) * 2 * nb].astype(jnp.float32)
                    turned = pltpu.roll(got, nb, 1)
                    for half in range(2):
                        place(plane_at((-b[0], -b[1])), 2 * q + half, half, got, turned)
        if 2 * group in FLIP:
            i = FLIP.index(2 * group)
            for dx, dc in line:
                copies["flip", i, dx, dc].wait_recv()
            for o in range(GROUPS):
                got = tin[i, o * nb : (o + 1) * nb, :].astype(jnp.float32)
                turned = pltpu.roll(got, nb, 1)
                for half in range(2):
                    place(plane_at(ROWS[2 * group + half]), o, half, got, turned)

    sent = []
    cost = [2 * 2 * nb * (chunk if k else width) / RATE for k in range(parts + 1)]
    links = transfers(parts, cost)
    steps = schedule(links)
    source = {name: link for link, order in links.items() for name, _, _ in order}

    def names(kind, k=None, blocks=None):
        return [n for n in source if n[0] == kind and k in (None, n[-1]) and (blocks is None or n[1] in blocks)]

    def columns(k):
        return names("col", k) + names("far", k) + names("sib", k)

    done = [0] * (len(ROWS) // 2)
    tasks = []
    for k in range(parts + 1):
        for group in range(len(ROWS) // 2):
            blocks = ROWS[2 * group : 2 * group + 2]
            need = names("row", k, blocks) + (columns(k) if k else names("y"))
            tasks.append((set(need), functools.partial(work, group, k)))

    seen = set()
    for _, start, name in steps:
        if start:
            pass_on(name)
            continue
        for copy in [copies["y", dx, dc] for dx, dc in line] if name == ("y",) else [copies[name]]:
            copy.wait_recv()
        seen.add(name)
        for task in [t for t in tasks if seen >= t[0]]:
            task[1]()
            tasks.remove(task)

    while sent:
        gather(sent.pop(0))
    for copy in copies.values():
        copy.wait_send()


def body(rho_x, rho_s, coulomb, screening, qmap, qslot):
    kpoints, npair, waves = rho_x.shape
    width = rho_s.shape[-1]
    nb = kpoints * npair
    parts = PARTS
    chunk = waves // parts
    cols = GROUPS * nb
    bf16, f32 = jnp.bfloat16, jnp.float32
    vmem = pl.BlockSpec(memory_space=pltpu.VMEM)
    hbm = pl.BlockSpec(memory_space=pltpu.HBM)
    ncopies = 15 + (9 + 4 + 4) * (parts + 1) + 7 + len(OUT) + 7 * len(FLIP)
    out = pl.pallas_call(
        functools.partial(kernel, parts),
        out_shape=jax.ShapeDtypeStruct((nb, GROUPS * PLANE * nb), bf16),
        in_specs=[hbm] * 6,
        out_specs=vmem,
        scratch_shapes=[
            pltpu.VMEM((nb, waves), bf16),
            pltpu.VMEM((waves,), f32),
            pltpu.SMEM(qmap.shape, jnp.int32),
            pltpu.SMEM(qslot.shape, jnp.int32),
            pltpu.VMEM((len(ROWS) * nb, width), bf16),
            pltpu.VMEM((parts, len(ROWS) * nb, chunk), bf16),
            pltpu.VMEM((cols, width), bf16),
            pltpu.VMEM((parts, cols, chunk), bf16),
            pltpu.VMEM((PLANE, nb, width), bf16),
            pltpu.VMEM((PLANE, nb, cols), bf16),
            pltpu.VMEM((GROUPS, nb, cols), bf16),
            pltpu.VMEM((width, cols), bf16),
            pltpu.VMEM((len(ROWS) * nb, cols), bf16),
            pltpu.VMEM((len(FLIP), cols, 2 * nb), bf16),
            pltpu.VMEM((len(FLIP), cols, 2 * nb), bf16),
            pltpu.VMEM((len(ROWS), nb, cols), bf16),
            pltpu.VMEM((len(ROWS) * nb, cols), f32),
            pltpu.SemaphoreType.DMA((7,)),
            pltpu.SemaphoreType.DMA((ncopies,)),
            pltpu.SemaphoreType.DMA((ncopies,)),
        ],
        compiler_params=pltpu.CompilerParams(
            collective_id=0, has_side_effects=True, vmem_limit_bytes=62 * 2**20
        ),
        name="kernel_rows",
    )(
        rho_x.reshape(nb, waves),
        rho_s.reshape(nb, width),
        coulomb,
        screening.reshape(width, width),
        qmap,
        qslot,
    )
    return out.astype(f32).reshape(kpoints, npair, -1)


def solution(mesh):
    placed = (
        P(("krow", "tri"), None, None),
        P(("krow", "tri"), None, None),
        P(),
        P("tri", None, None),
        P(),
        P(),
    )
    return jax.shard_map(
        body, mesh=mesh, in_specs=placed, out_specs=P(("krow", "tri"), None, None), check_vma=False
    )
```

```python
import functools

import jax
import jax.numpy as jnp
from jax import lax
from jax.experimental import pallas as pl
from jax.experimental.pallas import tpu as pltpu
from jax.sharding import PartitionSpec as P

MESH = pl.DeviceIdType.MESH
SIDE = 4
CORES = 2
GROUPS = SIDE * CORES
PLANE = SIDE * SIDE

ROWS = ((0, 0), (0, 2), (0, 1), (1, 0), (2, 0), (2, 2), (2, 3), (3, 1), (3, 2), (3, 3))
PLAN = {
    (0, 1): (
        (0, 1, 3), (0, 1, 1), (0, 2, 3), (1, 1, -1), (0, 1, 0), (0, 1, 2), (0, 2, 0), (0, 2, 1),
        (3, 3, 3), (3, 2, 2), (0, 2, 2), (3, 3, 1),
    ),
    (1, 0): (
        (1, 0, -1), (1, 0, 1), (1, 0, 2), (1, 2, -1), (1, 0, 0), (2, 0, 2), (2, 0, 0), (2, 0, 1),
        (1, 0, 3), (3, 3, 2), (2, 0, 3), (3, 3, 0),
    ),
    (0, 3): (
        (0, 3, -1), (0, 2, -1), (1, 3, -1), (3, 3, -1), (2, 3, -1), (0, 1, -1), (3, 1, -1), (2, 2, -1),
        (2, 3, 2), (2, 3, 0), (2, 3, 1), (2, 2, 0), (3, 1, 0), (2, 2, 1), (2, 2, 2),
    ),
    (3, 0): (
        (3, 0, -1), (2, 0, -1), (3, 1, 3), (3, 2, -1), (3, 1, 1), (3, 2, 3), (2, 1, -1), (3, 1, 2),
        (3, 2, 0), (3, 2, 1), (2, 2, 3), (2, 3, 3),
    ),
}
OUT = tuple(i for i, b in enumerate(ROWS) if b[0] % 2 or b[1] % 2)
FLIP = (0, 2, 4, 6, 8)
PARTS = 3
RATE = 8e4
LATENCY = 1.9
WINDOW = 3


def less(b, e):
    return ((b[0] - e[0]) % SIDE, (b[1] - e[1]) % SIDE)


def transfers(parts, cost):
    links = {}
    for e, entries in PLAN.items():
        links[e] = []
        for dy, dz, k in entries:
            kind, rest = ("w", ()) if k < 0 else ("row", (k,))
            parent = (kind, less((dy, dz), e)) + rest
            need = [parent] if parent[1] != (0, 0) else []
            links[e].append(((kind, (dy, dz)) + rest, cost[0] if k < 0 else cost[k], need))
    for dx in (1, 3):
        order = []
        for k in range(parts + 1):
            order.append((("col", dx, k), cost[k], []))
            if k:
                order.append((("far", dx, k - 1), cost[k - 1] / 2, [("col", dx, k - 1)]))
        links[dx] = order + [(("far", dx, parts), cost[parts] / 2, [("col", dx, parts)])]
    links["sib"] = []
    for k in range(parts + 1):
        for dx in (0, 1, 3, 2):
            need = {0: [], 1: [("col", 1, k)], 3: [("col", 3, k)], 2: [("far", 1, k), ("far", 3, k)]}[dx]
            links["sib"].append((("sib", dx, k), cost[k] / 6, need))
    early = [n for v in links.values() for n, _, _ in v if n[0] == "w" or n[0] in ("col", "far", "sib") and n[-1] == 0]
    links["y"] = [(("y",), 6.0, early)]
    return links


def schedule(links):
    arrive, at, free, steps = {}, dict.fromkeys(links, 0), dict.fromkeys(links, 0.0), []
    while any(at[link] < len(links[link]) for link in links):
        for link, order in links.items():
            while at[link] < len(order) and all(n in arrive for n in order[at[link]][2]):
                name, cost, need = order[at[link]]
                ready = max([arrive[n] for n in need], default=0.0)
                paced = arrive[order[at[link] - WINDOW][0]] if at[link] >= WINDOW else 0.0
                free[link] = max(free[link], ready) + cost
                arrive[name] = free[link] + LATENCY
                steps += [(max(ready, paced), 1, name), (arrive[name], 0, name)]
                at[link] += 1
    return sorted(steps, key=lambda v: v[:2])


def kernel(parts, rx_hbm, rs_hbm, cou_hbm, w_hbm, qmap_hbm, qslot_hbm, out,
           rx, cou, qmap, qslot, srow, xrow, scol, xcol, wst, pt, ysend, y, rout, tout, tin, inb, acc,
           lsem, ssem, rsem):
    width = srow.shape[1]
    nb = rx.shape[0]
    chunk = xrow.shape[2]
    kr = lax.axis_index("krow")
    tr = lax.axis_index("tri")
    px, pc = kr // CORES, kr % CORES
    pz, py = tr // SIDE, tr % SIDE

    def plane_at(b):
        return ((pz + b[1]) % SIDE) * SIDE + (py + b[0]) % SIDE

    def line_at(dx, dc):
        return ((px + dx) % SIDE) * CORES + (pc + dc) % CORES

    def block(index):
        return pl.ds(pl.multiple_of(index * nb, nb), nb)

    def row(k, slot):
        rows = pl.ds(slot * nb, nb)
        return srow.at[rows] if k == 0 else xrow.at[k - 1, rows]

    def col(k, o):
        return scol.at[block(o)] if k == 0 else xcol.at[k - 1, block(o)]

    line = [(dx, dc) for dx in range(SIDE) for dc in range(CORES) if (dx, dc) != (0, 0)]
    others = [(dy, dz) for dy in range(SIDE) for dz in range(SIDE) if (dy, dz) != (0, 0)]

    barrier = pltpu.get_barrier_semaphore()
    for b in others:
        pl.semaphore_signal(barrier, inc=1, device_id={"tri": plane_at(b)}, device_id_type=MESH)
    for dx, dc in line:
        pl.semaphore_signal(barrier, inc=1, device_id={"krow": line_at(dx, dc)}, device_id_type=MESH)

    loads = [
        pltpu.make_async_copy(src, dst, lsem.at[i])
        for i, (src, dst) in enumerate((
            (rx_hbm, rx), (cou_hbm, cou), (rs_hbm, srow.at[0:nb]), (rs_hbm, scol.at[block(kr)]),
            (w_hbm.at[block(kr)], wst.at[tr]), (qmap_hbm, qmap), (qslot_hbm, qslot),
        ))
    ]
    for load in loads:
        load.start()

    def scale(k):
        if not scaled:
            loads[0].wait()
            loads[1].wait()
        scaled.add(k)
        lanes = pl.ds((k - 1) * chunk, chunk)
        own = (rx[:, lanes].astype(jnp.float32) * jnp.sqrt(cou[lanes]).reshape(1, chunk)).astype(jnp.bfloat16)
        xrow[k - 1, 0:nb, :] = own
        xcol[k - 1, block(kr), :] = own

    out[...] = jnp.zeros_like(out)
    pl.semaphore_wait(barrier, len(others) + len(line))

    copies = {}

    def send(name, src, dst, device):
        i = len(copies)
        copies[name] = pltpu.make_async_remote_copy(
            src_ref=src, dst_ref=dst, send_sem=ssem.at[i], recv_sem=rsem.at[i],
            device_id=device, device_id_type=MESH,
        )
        copies[name].start()

    scaled = set()

    def pass_on(name):
        kind = name[0]
        if kind in ("row", "col") and name[-1] not in scaled | {0}:
            scale(name[-1])
        if kind == "w":
            b, e = name[1], source[name]
            held = wst.at[plane_at(less(b, e))]
            own = w_hbm.at[block(kr)] if less(b, e) == (0, 0) else held
            send(name, own, held, {"tri": plane_at((-e[0], -e[1]))})
        elif kind == "row":
            b, k = name[1:]
            e = source[name]
            own = rs_hbm if k == 0 and less(b, e) == (0, 0) else row(k, ROWS.index(less(b, e)))
            send(name, own, row(k, ROWS.index(b)), {"tri": plane_at((-e[0], -e[1]))})
        elif kind == "col":
            dx, k = name[1:]
            send(name, col(k, kr) if k else rs_hbm, col(k, kr), {"krow": line_at(-dx, 0)})
        elif kind == "far":
            dx, k = name[1:]
            held = col(k, line_at(dx, 0)).at[pl.ds(0 if dx == 1 else nb // 2, nb // 2)]
            send(name, held, held, {"krow": line_at(-dx, 0)})
        elif kind == "sib":
            dx, k = name[1:]
            held = col(k, line_at(dx, 0))
            send(name, rs_hbm if (dx, k) == (0, 0) else held, held, {"krow": line_at(0, 1)})
        else:
            project()

    def project():
        for load in loads[2:]:
            load.wait()
        pt[...] = (
            lax.dot_general(
                wst[...].reshape(PLANE * nb, width), scol[...], (((1,), (1,)), ((), ())),
                preferred_element_type=jnp.float32,
            ) * -0.5
        ).astype(jnp.bfloat16).reshape(pt.shape)
        low = lax.broadcasted_iota(jnp.int32, (nb, 2 * nb), 1) < nb
        for dx, dc in line + [(0, 0)]:
            o = line_at(dx, dc)
            for q in range(GROUPS // 2):
                lanes = pl.ds(q * 2 * nb, 2 * nb)
                first = pt[qslot[qmap[o, 2 * q]], :, lanes]
                second = pt[qslot[qmap[o, 2 * q + 1]], :, lanes]
                ysend[o, :, lanes] = jnp.where(low, first, second)
            if (dx, dc) == (0, 0):
                y[block(kr), :] = ysend[kr]
            else:
                send(("y", dx, dc), ysend.at[o], y.at[block(kr)], {"krow": o})

    def rows_of(group):
        return slice(group * 2 * nb, (group + 1) * 2 * nb)

    def work(group, k):
        rows = rows_of(group)
        if k == 0:
            part = jnp.dot(srow[rows, :], y[...], preferred_element_type=jnp.float32)
        else:
            part = lax.dot_general(
                xrow[k - 1, rows, :], xcol[k - 1], (((1,), (1,)), ((), ())), preferred_element_type=jnp.float32
            )
        total = part if not done[group] else acc[rows, :] + part
        done[group] += 1
        if done[group] <= parts:
            acc[rows, :] = total
        else:
            finish(group, total)

    def finish(group, total):
        rows = rows_of(group)
        total = total * 2.0
        rout[rows, :] = total.astype(jnp.bfloat16)
        for slot in (2 * group, 2 * group + 1):
            b = ROWS[slot]
            if slot in OUT:
                send(("out", b), rout.at[pl.ds(slot * nb, nb)], inb.at[slot], {"tri": plane_at(b)})
        if 2 * group in FLIP:
            i = FLIP.index(2 * group)
            tout[i] = total.T.astype(jnp.bfloat16)
            for dx, dc in line:
                o = line_at(dx, dc)
                send(("flip", i, dx, dc), tout.at[i, block(o)], tin.at[i, block(kr)], {"krow": o})
            tin[i, block(kr), :] = tout[i, block(kr), :]
        sent.append(group)

    upper = lax.broadcasted_iota(jnp.int32, (nb, 2 * nb), 1) // nb
    span = PLANE * nb

    def place(t, o, half, got, turned):
        lanes = pl.ds(pl.multiple_of(o * span + (t // 2) * 2 * nb, 2 * nb), 2 * nb)
        value = jnp.where(t % 2 == half, got, turned)
        out[:, lanes] = jnp.where(upper == t % 2, value, out[:, lanes].astype(jnp.float32)).astype(out.dtype)

    def gather(group):
        for slot in (2 * group, 2 * group + 1):
            if slot in OUT or slot == 0:
                b = ROWS[slot]
                if slot:
                    copies["out", b].wait_recv()
                held = inb.at[slot] if slot else rout.at[0:nb]
                for q in range(GROUPS // 2):
                    got = held[:, q * 2 * nb : (q + 1) * 2 * nb].astype(jnp.float32)
                    turned = pltpu.roll(got, nb, 1)
                    for half in range(2):
                        place(plane_at((-b[0], -b[1])), 2 * q + half, half, got, turned)
        if 2 * group in FLIP:
            i = FLIP.index(2 * group)
            for dx, dc in line:
                copies["flip", i, dx, dc].wait_recv()
            for o in range(GROUPS):
                got = tin[i, o * nb : (o + 1) * nb, :].astype(jnp.float32)
                turned = pltpu.roll(got, nb, 1)
                for half in range(2):
                    if 2 * group + half:
                        place(plane_at(ROWS[2 * group + half]), o, half, got, turned)

    sent = []
    cost = [2 * 2 * nb * (chunk if k else width) / RATE for k in range(parts + 1)]
    links = transfers(parts, cost)
    steps = schedule(links)
    source = {name: link for link, order in links.items() for name, _, _ in order}

    def names(kind, k=None, blocks=None):
        return [n for n in source if n[0] == kind and k in (None, n[-1]) and (blocks is None or n[1] in blocks)]

    def columns(k):
        return names("col", k) + names("far", k) + names("sib", k)

    done = [0] * (len(ROWS) // 2)
    tasks = []
    for k in range(parts + 1):
        for group in range(len(ROWS) // 2):
            blocks = ROWS[2 * group : 2 * group + 2]
            need = names("row", k, blocks) + (columns(k) if k else names("y"))
            tasks.append((set(need), functools.partial(work, group, k)))

    seen = set()
    for _, start, name in steps:
        if start:
            pass_on(name)
            continue
        for copy in [copies["y", dx, dc] for dx, dc in line] if name == ("y",) else [copies[name]]:
            copy.wait_recv()
        seen.add(name)
        for task in [t for t in tasks if seen >= t[0]]:
            task[1]()
            tasks.remove(task)

    while sent:
        gather(sent.pop(0))
    for copy in copies.values():
        copy.wait_send()


def widen(pieces, src, dst, held, wide, sem_in, sem_out):
    rows = src.shape[0] // pieces
    reads = [pltpu.make_async_copy(src.at[pl.ds(i * rows, rows)], held.at[pl.ds(i * rows, rows)], sem_in.at[i]) for i in range(pieces)]
    writes = [pltpu.make_async_copy(wide.at[pl.ds(i * rows, rows)], dst.at[pl.ds(i * rows, rows)], sem_out.at[i]) for i in range(pieces)]
    for read in reads:
        read.start()
    for i in range(pieces):
        reads[i].wait()
        wide[i * rows : (i + 1) * rows, :] = held[i * rows : (i + 1) * rows, :].astype(wide.dtype)
        writes[i].start()
    for write in writes:
        write.wait()


def body(rho_x, rho_s, coulomb, screening, qmap, qslot):
    kpoints, npair, waves = rho_x.shape
    width = rho_s.shape[-1]
    nb = kpoints * npair
    parts = PARTS
    chunk = waves // parts
    cols = GROUPS * nb
    bf16, f32 = jnp.bfloat16, jnp.float32
    vmem = pl.BlockSpec(memory_space=pltpu.VMEM)
    hbm = pl.BlockSpec(memory_space=pltpu.HBM)
    ncopies = 15 + (9 + 4 + 4) * (parts + 1) + 7 + len(OUT) + 7 * len(FLIP)
    out = pl.pallas_call(
        functools.partial(kernel, parts),
        out_shape=jax.ShapeDtypeStruct((nb, GROUPS * PLANE * nb), bf16),
        in_specs=[hbm] * 6,
        out_specs=vmem,
        scratch_shapes=[
            pltpu.VMEM((nb, waves), bf16),
            pltpu.VMEM((waves,), f32),
            pltpu.SMEM(qmap.shape, jnp.int32),
            pltpu.SMEM(qslot.shape, jnp.int32),
            pltpu.VMEM((len(ROWS) * nb, width), bf16),
            pltpu.VMEM((parts, len(ROWS) * nb, chunk), bf16),
            pltpu.VMEM((cols, width), bf16),
            pltpu.VMEM((parts, cols, chunk), bf16),
            pltpu.VMEM((PLANE, nb, width), bf16),
            pltpu.VMEM((PLANE, nb, cols), bf16),
            pltpu.VMEM((GROUPS, nb, cols), bf16),
            pltpu.VMEM((width, cols), bf16),
            pltpu.VMEM((len(ROWS) * nb, cols), bf16),
            pltpu.VMEM((len(FLIP), cols, 2 * nb), bf16),
            pltpu.VMEM((len(FLIP), cols, 2 * nb), bf16),
            pltpu.VMEM((len(ROWS), nb, cols), bf16),
            pltpu.VMEM((len(ROWS) * nb, cols), f32),
            pltpu.SemaphoreType.DMA((7,)),
            pltpu.SemaphoreType.DMA((ncopies,)),
            pltpu.SemaphoreType.DMA((ncopies,)),
        ],
        compiler_params=pltpu.CompilerParams(
            collective_id=0, has_side_effects=True, vmem_limit_bytes=62 * 2**20
        ),
        name="kernel_rows",
    )(
        rho_x.reshape(nb, waves),
        rho_s.reshape(nb, width),
        coulomb,
        screening.reshape(width, width),
        qmap,
        qslot,
    )
    pieces = 4
    out = pl.pallas_call(
        functools.partial(widen, pieces),
        out_shape=jax.ShapeDtypeStruct(out.shape, f32),
        in_specs=[hbm],
        out_specs=hbm,
        scratch_shapes=[
            pltpu.VMEM(out.shape, bf16),
            pltpu.VMEM(out.shape, f32),
            pltpu.SemaphoreType.DMA((pieces,)),
            pltpu.SemaphoreType.DMA((pieces,)),
        ],
        compiler_params=pltpu.CompilerParams(vmem_limit_bytes=62 * 2**20),
        name="widen",
    )(out)
    return out.reshape(kpoints, npair, -1)


def solution(mesh):
    placed = (
        P(("krow", "tri"), None, None),
        P(("krow", "tri"), None, None),
        P(),
        P("tri", None, None),
        P(),
        P(),
    )
    return jax.shard_map(
        body, mesh=mesh, in_specs=placed, out_specs=P(("krow", "tri"), None, None), check_vma=False
    )
```

```python
import functools

import jax
import jax.numpy as jnp
from jax import lax
from jax.experimental import pallas as pl
from jax.experimental.pallas import tpu as pltpu
from jax.sharding import PartitionSpec as P

MESH = pl.DeviceIdType.MESH
SIDE = 4
CORES = 2
GROUPS = SIDE * CORES
PLANE = SIDE * SIDE

ROWS = ((0, 0), (0, 2), (0, 1), (1, 0), (2, 0), (2, 2), (2, 3), (3, 1), (3, 2), (3, 3))
PLAN = {
    (0, 1): (
        (0, 1, 3), (0, 1, 1), (0, 2, 3), (1, 1, -1), (0, 1, 0), (0, 1, 2), (0, 2, 0), (0, 2, 1),
        (3, 3, 3), (3, 2, 2), (0, 2, 2), (3, 3, 1),
    ),
    (1, 0): (
        (1, 0, -1), (1, 0, 1), (1, 0, 2), (1, 2, -1), (1, 0, 0), (2, 0, 2), (2, 0, 0), (2, 0, 1),
        (1, 0, 3), (3, 3, 2), (2, 0, 3), (3, 3, 0),
    ),
    (0, 3): (
        (0, 3, -1), (0, 2, -1), (1, 3, -1), (3, 3, -1), (2, 3, -1), (0, 1, -1), (3, 1, -1), (2, 2, -1),
        (2, 3, 2), (2, 3, 0), (2, 3, 1), (2, 2, 0), (3, 1, 0), (2, 2, 1), (2, 2, 2),
    ),
    (3, 0): (
        (3, 0, -1), (2, 0, -1), (3, 1, 3), (3, 2, -1), (3, 1, 1), (3, 2, 3), (2, 1, -1), (3, 1, 2),
        (3, 2, 0), (3, 2, 1), (2, 2, 3), (2, 3, 3),
    ),
}
OUT = tuple(i for i, b in enumerate(ROWS) if b[0] % 2 or b[1] % 2)
FLIP = (0, 2, 4, 6, 8)
PARTS = 3
RATE = 8e4
LATENCY = 1.9
WINDOW = 3


def less(b, e):
    return ((b[0] - e[0]) % SIDE, (b[1] - e[1]) % SIDE)


def transfers(parts, cost):
    links = {}
    for e, entries in PLAN.items():
        links[e] = []
        for dy, dz, k in entries:
            kind, rest = ("w", ()) if k < 0 else ("row", (k,))
            parent = (kind, less((dy, dz), e)) + rest
            need = [parent] if parent[1] != (0, 0) else []
            links[e].append(((kind, (dy, dz)) + rest, cost[0] if k < 0 else cost[k], need))
    for dx in (1, 3):
        order = []
        for k in range(parts + 1):
            order.append((("col", dx, k), cost[k], []))
            if k:
                order.append((("far", dx, k - 1), cost[k - 1] / 2, [("col", dx, k - 1)]))
        links[dx] = order + [(("far", dx, parts), cost[parts] / 2, [("col", dx, parts)])]
    links["sib"] = []
    for k in range(parts + 1):
        for dx in (0, 1, 3, 2):
            need = {0: [], 1: [("col", 1, k)], 3: [("col", 3, k)], 2: [("far", 1, k), ("far", 3, k)]}[dx]
            links["sib"].append((("sib", dx, k), cost[k] / 6, need))
    early = [n for v in links.values() for n, _, _ in v if n[0] == "w" or n[0] in ("col", "far", "sib") and n[-1] == 0]
    links["y"] = [(("y",), 6.0, early)]
    return links


def schedule(links):
    arrive, at, free, steps = {}, dict.fromkeys(links, 0), dict.fromkeys(links, 0.0), []
    while any(at[link] < len(links[link]) for link in links):
        for link, order in links.items():
            while at[link] < len(order) and all(n in arrive for n in order[at[link]][2]):
                name, cost, need = order[at[link]]
                ready = max([arrive[n] for n in need], default=0.0)
                depth = WINDOW + (name[-1] == 0 or name[0] == "w")
                paced = arrive[order[at[link] - depth][0]] if at[link] >= depth else 0.0
                free[link] = max(free[link], ready) + cost
                arrive[name] = free[link] + LATENCY
                steps += [(max(ready, paced), 1, name), (arrive[name], 0, name)]
                at[link] += 1
    return sorted(steps, key=lambda v: v[:2])


def kernel(parts, rx_hbm, rs_hbm, cou_hbm, w_hbm, qmap_hbm, qslot_hbm, inb,
           rx, cou, qmap, qslot, srow, xrow, scol, xcol, wst, pt, ysend, y, rout, tout, tin, acc,
           lsem, ssem, rsem):
    width = srow.shape[1]
    nb = rx.shape[0]
    chunk = xrow.shape[2]
    kr = lax.axis_index("krow")
    tr = lax.axis_index("tri")
    px, pc = kr // CORES, kr % CORES
    pz, py = tr // SIDE, tr % SIDE

    def plane_at(b):
        return ((pz + b[1]) % SIDE) * SIDE + (py + b[0]) % SIDE

    def line_at(dx, dc):
        return ((px + dx) % SIDE) * CORES + (pc + dc) % CORES

    def block(index):
        return pl.ds(pl.multiple_of(index * nb, nb), nb)

    def row(k, slot):
        rows = pl.ds(slot * nb, nb)
        return srow.at[rows] if k == 0 else xrow.at[k - 1, rows]

    def col(k, o):
        return scol.at[block(o)] if k == 0 else xcol.at[k - 1, block(o)]

    line = [(dx, dc) for dx in range(SIDE) for dc in range(CORES) if (dx, dc) != (0, 0)]
    others = [(dy, dz) for dy in range(SIDE) for dz in range(SIDE) if (dy, dz) != (0, 0)]

    barrier = pltpu.get_barrier_semaphore()
    for b in others:
        pl.semaphore_signal(barrier, inc=1, device_id={"tri": plane_at(b)}, device_id_type=MESH)
    for dx, dc in line:
        pl.semaphore_signal(barrier, inc=1, device_id={"krow": line_at(dx, dc)}, device_id_type=MESH)

    loads = [
        pltpu.make_async_copy(src, dst, lsem.at[i])
        for i, (src, dst) in enumerate((
            (rx_hbm, rx), (cou_hbm, cou), (rs_hbm, srow.at[0:nb]), (rs_hbm, scol.at[block(kr)]),
            (w_hbm.at[block(kr)], wst.at[tr]), (qmap_hbm, qmap), (qslot_hbm, qslot),
        ))
    ]
    for load in loads:
        load.start()

    def scale(k):
        if not scaled:
            loads[0].wait()
            loads[1].wait()
        scaled.add(k)
        lanes = pl.ds((k - 1) * chunk, chunk)
        own = (rx[:, lanes].astype(jnp.float32) * jnp.sqrt(cou[lanes]).reshape(1, chunk)).astype(jnp.bfloat16)
        xrow[k - 1, 0:nb, :] = own
        xcol[k - 1, block(kr), :] = own

    pl.semaphore_wait(barrier, len(others) + len(line))

    copies = {}

    def send(name, src, dst, device):
        i = len(copies)
        copies[name] = pltpu.make_async_remote_copy(
            src_ref=src, dst_ref=dst, send_sem=ssem.at[i], recv_sem=rsem.at[i],
            device_id=device, device_id_type=MESH,
        )
        copies[name].start()

    scaled = set()

    def pass_on(name):
        kind = name[0]
        if kind in ("row", "col") and name[-1] not in scaled | {0}:
            scale(name[-1])
        if kind == "w":
            b, e = name[1], source[name]
            held = wst.at[plane_at(less(b, e))]
            own = w_hbm.at[block(kr)] if less(b, e) == (0, 0) else held
            send(name, own, held, {"tri": plane_at((-e[0], -e[1]))})
        elif kind == "row":
            b, k = name[1:]
            e = source[name]
            own = rs_hbm if k == 0 and less(b, e) == (0, 0) else row(k, ROWS.index(less(b, e)))
            send(name, own, row(k, ROWS.index(b)), {"tri": plane_at((-e[0], -e[1]))})
        elif kind == "col":
            dx, k = name[1:]
            send(name, col(k, kr) if k else rs_hbm, col(k, kr), {"krow": line_at(-dx, 0)})
        elif kind == "far":
            dx, k = name[1:]
            held = col(k, line_at(dx, 0)).at[pl.ds(0 if dx == 1 else nb // 2, nb // 2)]
            send(name, held, held, {"krow": line_at(-dx, 0)})
        elif kind == "sib":
            dx, k = name[1:]
            held = col(k, line_at(dx, 0))
            send(name, rs_hbm if (dx, k) == (0, 0) else held, held, {"krow": line_at(0, 1)})
        else:
            project()

    def project():
        for load in loads[2:]:
            load.wait()
        pt[...] = (
            lax.dot_general(
                wst[...].reshape(PLANE * nb, width), scol[...], (((1,), (1,)), ((), ())),
                preferred_element_type=jnp.float32,
            ) * -0.5
        ).astype(jnp.bfloat16).reshape(pt.shape)
        low = lax.broadcasted_iota(jnp.int32, (nb, 2 * nb), 1) < nb
        for dx, dc in line + [(0, 0)]:
            o = line_at(dx, dc)
            for q in range(GROUPS // 2):
                lanes = pl.ds(q * 2 * nb, 2 * nb)
                first = pt[qslot[qmap[o, 2 * q]], :, lanes]
                second = pt[qslot[qmap[o, 2 * q + 1]], :, lanes]
                ysend[o, :, lanes] = jnp.where(low, first, second)
            if (dx, dc) == (0, 0):
                y[block(kr), :] = ysend[kr]
            else:
                send(("y", dx, dc), ysend.at[o], y.at[block(kr)], {"krow": o})

    def rows_of(group):
        return slice(group * 2 * nb, (group + 1) * 2 * nb)

    def work(group, k):
        rows = rows_of(group)
        if k == 0:
            part = jnp.dot(srow[rows, :], y[...], preferred_element_type=jnp.float32)
        else:
            part = lax.dot_general(
                xrow[k - 1, rows, :], xcol[k - 1], (((1,), (1,)), ((), ())), preferred_element_type=jnp.float32
            )
        total = part if not done[group] else acc[rows, :] + part
        done[group] += 1
        if done[group] <= parts:
            acc[rows, :] = total
        else:
            finish(group, total)

    def finish(group, total):
        rows = rows_of(group)
        total = total * 2.0
        if 2 * group in FLIP:
            i = FLIP.index(2 * group)
            tout[i] = total.T.astype(jnp.bfloat16)
            for dx, dc in line:
                o = line_at(dx, dc)
                send(("flip", i, dx, dc), tout.at[i, block(o)], tin.at[i, block(kr)], {"krow": o})
            tin[i, block(kr), :] = tout[i, block(kr), :]
        rout[rows, :] = total.astype(jnp.bfloat16)
        for slot in (2 * group, 2 * group + 1):
            b = ROWS[slot]
            if slot in OUT:
                send(("out", b), rout.at[pl.ds(slot * nb, nb)], inb.at[tr], {"tri": plane_at(b)})
        sent.append(group)

    def gather(group):
        if group == 0:
            inb[tr] = rout[0:nb, :]
        if 2 * group in FLIP:
            i = FLIP.index(2 * group)
            for dx, dc in line:
                copies["flip", i, dx, dc].wait_recv()
            for q in range(GROUPS // 2):
                got = mix(tin[i, 2 * q * nb : (2 * q + 1) * nb, :], tin[i, (2 * q + 1) * nb : (2 * q + 2) * nb, :])
                for half in range(2):
                    if 2 * group + half:
                        inb[plane_at(ROWS[2 * group + half]), :, q * 2 * nb : (q + 1) * 2 * nb] = got[half].astype(inb.dtype)

    sent = []
    cost = [2 * 2 * nb * (chunk if k else width) / RATE for k in range(parts + 1)]
    links = transfers(parts, cost)
    steps = schedule(links)
    source = {name: link for link, order in links.items() for name, _, _ in order}

    def names(kind, k=None, blocks=None):
        return [n for n in source if n[0] == kind and k in (None, n[-1]) and (blocks is None or n[1] in blocks)]

    def columns(k):
        return names("col", k) + names("far", k) + names("sib", k)

    done = [0] * (len(ROWS) // 2)
    tasks = []
    for k in range(parts + 1):
        for group in range(len(ROWS) // 2):
            blocks = ROWS[2 * group : 2 * group + 2]
            need = names("row", k, blocks) + (columns(k) if k else names("y"))
            tasks.append((set(need), functools.partial(work, group, k)))

    seen = set()
    for _, start, name in steps:
        if start:
            pass_on(name)
            continue
        for copy in [copies["y", dx, dc] for dx, dc in line] if name == ("y",) else [copies[name]]:
            copy.wait_recv()
        seen.add(name)
        for task in [t for t in tasks if seen >= t[0]]:
            task[1]()
            tasks.remove(task)

    while sent:
        gather(sent.pop(0))
    for slot in OUT:
        copies["out", ROWS[slot]].wait_recv()
    for copy in copies.values():
        copy.wait_send()


def mix(first, second):
    nb = first.shape[0]
    low = lax.broadcasted_iota(jnp.int32, first.shape, 1) < nb
    first, second = first.astype(jnp.float32), second.astype(jnp.float32)
    return jnp.where(low, first, pltpu.roll(second, nb, 1)), jnp.where(low, pltpu.roll(first, nb, 1), second)


def widen(src, dst, held, wide, sem_in, sem_out):
    pieces, plane, nb, tile = held.shape
    span = plane * nb
    reads = [
        pltpu.make_async_copy(src.at[:, :, pl.ds(q * tile, tile)], held.at[q], sem_in.at[q]) for q in range(pieces)
    ]
    writes = [
        pltpu.make_async_copy(wide.at[q], dst.at[:, pl.ds(q * 2 * span, 2 * span)], sem_out.at[q]) for q in range(pieces)
    ]
    for read in reads:
        read.start()
    for q in range(pieces):
        reads[q].wait()
        for m in range(plane // 2):
            for half, got in enumerate(mix(held[q, 2 * m], held[q, 2 * m + 1])):
                at = half * span + m * tile
                wide[q, :, at : at + tile] = got
        writes[q].start()
    for write in writes:
        write.wait()


def body(rho_x, rho_s, coulomb, screening, qmap, qslot):
    kpoints, npair, waves = rho_x.shape
    width = rho_s.shape[-1]
    nb = kpoints * npair
    parts = PARTS
    chunk = waves // parts
    cols = GROUPS * nb
    bf16, f32 = jnp.bfloat16, jnp.float32
    vmem = pl.BlockSpec(memory_space=pltpu.VMEM)
    hbm = pl.BlockSpec(memory_space=pltpu.HBM)
    ncopies = 15 + (9 + 4 + 4) * (parts + 1) + 7 + len(OUT) + 7 * len(FLIP)
    out = pl.pallas_call(
        functools.partial(kernel, parts),
        out_shape=jax.ShapeDtypeStruct((PLANE, nb, cols), bf16),
        in_specs=[hbm] * 6,
        out_specs=vmem,
        scratch_shapes=[
            pltpu.VMEM((nb, waves), bf16),
            pltpu.VMEM((waves,), f32),
            pltpu.SMEM(qmap.shape, jnp.int32),
            pltpu.SMEM(qslot.shape, jnp.int32),
            pltpu.VMEM((len(ROWS) * nb, width), bf16),
            pltpu.VMEM((parts, len(ROWS) * nb, chunk), bf16),
            pltpu.VMEM((cols, width), bf16),
            pltpu.VMEM((parts, cols, chunk), bf16),
            pltpu.VMEM((PLANE, nb, width), bf16),
            pltpu.VMEM((PLANE, nb, cols), bf16),
            pltpu.VMEM((GROUPS, nb, cols), bf16),
            pltpu.VMEM((width, cols), bf16),
            pltpu.VMEM((len(ROWS) * nb, cols), bf16),
            pltpu.VMEM((len(FLIP), cols, 2 * nb), bf16),
            pltpu.VMEM((len(FLIP), cols, 2 * nb), bf16),
            pltpu.VMEM((len(ROWS) * nb, cols), f32),
            pltpu.SemaphoreType.DMA((7,)),
            pltpu.SemaphoreType.DMA((ncopies,)),
            pltpu.SemaphoreType.DMA((ncopies,)),
        ],
        compiler_params=pltpu.CompilerParams(
            collective_id=0, has_side_effects=True, vmem_limit_bytes=62 * 2**20
        ),
        name="kernel_rows",
    )(
        rho_x.reshape(nb, waves),
        rho_s.reshape(nb, width),
        coulomb,
        screening.reshape(width, width),
        qmap,
        qslot,
    )
    pieces = GROUPS // 2
    out = pl.pallas_call(
        widen,
        out_shape=jax.ShapeDtypeStruct((nb, PLANE * cols), f32),
        in_specs=[hbm],
        out_specs=hbm,
        scratch_shapes=[
            pltpu.VMEM((pieces, PLANE, nb, 2 * nb), bf16),
            pltpu.VMEM((pieces, nb, PLANE * cols // pieces), f32),
            pltpu.SemaphoreType.DMA((pieces,)),
            pltpu.SemaphoreType.DMA((pieces,)),
        ],
        compiler_params=pltpu.CompilerParams(vmem_limit_bytes=62 * 2**20),
        name="widen",
    )(out)
    return out.reshape(kpoints, npair, -1)


def solution(mesh):
    placed = (
        P(("krow", "tri"), None, None),
        P(("krow", "tri"), None, None),
        P(),
        P("tri", None, None),
        P(),
        P(),
    )
    return jax.shard_map(
        body, mesh=mesh, in_specs=placed, out_specs=P(("krow", "tri"), None, None), check_vma=False
    )
```

```python
import functools

import jax
import jax.numpy as jnp
from jax import lax
from jax.experimental import pallas as pl
from jax.experimental.pallas import tpu as pltpu
from jax.sharding import PartitionSpec as P

MESH = pl.DeviceIdType.MESH
SIDE = 4
CORES = 2
GROUPS = SIDE * CORES
PLANE = SIDE * SIDE

ROWS = ((0, 0), (0, 2), (0, 1), (1, 0), (2, 0), (2, 2), (2, 3), (3, 1), (3, 2), (3, 3))
PLAN = {
    (0, 1): (
        (0, 1, 3), (0, 1, 1), (0, 2, 3), (1, 1, -1), (0, 1, 0), (0, 1, 2), (0, 2, 0), (0, 2, 1),
        (3, 3, 3), (3, 2, 2), (0, 2, 2), (3, 3, 1),
    ),
    (1, 0): (
        (1, 0, -1), (1, 0, 1), (1, 0, 2), (1, 2, -1), (1, 0, 0), (2, 0, 2), (2, 0, 0), (2, 0, 1),
        (1, 0, 3), (3, 3, 2), (2, 0, 3), (3, 3, 0),
    ),
    (0, 3): (
        (0, 3, -1), (0, 2, -1), (1, 3, -1), (3, 3, -1), (2, 3, -1), (0, 1, -1), (3, 1, -1), (2, 2, -1),
        (2, 3, 2), (2, 3, 0), (2, 3, 1), (2, 2, 0), (3, 1, 0), (2, 2, 1), (2, 2, 2),
    ),
    (3, 0): (
        (3, 0, -1), (2, 0, -1), (3, 1, 3), (3, 2, -1), (3, 1, 1), (3, 2, 3), (2, 1, -1), (3, 1, 2),
        (3, 2, 0), (3, 2, 1), (2, 2, 3), (2, 3, 3),
    ),
}
OUT = tuple(i for i, b in enumerate(ROWS) if b[0] % 2 or b[1] % 2)
FLIP = (0, 2, 4, 6, 8)
PARTS = 3
RATE = 8e4
LATENCY = 1.9
WINDOW = 3


def less(b, e):
    return ((b[0] - e[0]) % SIDE, (b[1] - e[1]) % SIDE)


def transfers(parts, cost):
    links = {}
    for e, entries in PLAN.items():
        links[e] = []
        for dy, dz, k in entries:
            kind, rest = ("w", ()) if k < 0 else ("row", (k,))
            parent = (kind, less((dy, dz), e)) + rest
            need = [parent] if parent[1] != (0, 0) else []
            links[e].append(((kind, (dy, dz)) + rest, cost[0] if k < 0 else cost[k], need))
    for dx in (1, 3):
        order = []
        for k in range(parts + 1):
            order.append((("col", dx, k), cost[k], []))
            if k:
                order.append((("far", dx, k - 1), cost[k - 1] / 2, [("col", dx, k - 1)]))
        links[dx] = order + [(("far", dx, parts), cost[parts] / 2, [("col", dx, parts)])]
    links["sib"] = []
    for k in range(parts + 1):
        for dx in (0, 1, 3, 2):
            need = {0: [], 1: [("col", 1, k)], 3: [("col", 3, k)], 2: [("far", 1, k), ("far", 3, k)]}[dx]
            links["sib"].append((("sib", dx, k), cost[k] / 6, need))
    early = [n for v in links.values() for n, _, _ in v if n[0] == "w" or n[0] in ("col", "far", "sib") and n[-1] == 0]
    links["y"] = [(("y",), 6.0, early)]
    return links


def schedule(links):
    arrive, at, free, steps = {}, dict.fromkeys(links, 0), dict.fromkeys(links, 0.0), []
    while any(at[link] < len(links[link]) for link in links):
        for link, order in links.items():
            while at[link] < len(order) and all(n in arrive for n in order[at[link]][2]):
                name, cost, need = order[at[link]]
                ready = max([arrive[n] for n in need], default=0.0)
                before = [n for n, _, _ in order[: at[link]] if n[0] != "w"]
                depth = WINDOW + (name[-1] == 0)
                paced = arrive[before[-depth]] if len(before) >= depth and name[0] != "w" else 0.0
                free[link] = max(free[link], ready) + cost
                arrive[name] = free[link] + LATENCY
                steps += [(max(ready, paced), 1, name), (arrive[name], 0, name)]
                at[link] += 1
    return sorted(steps, key=lambda v: v[:2])


def kernel(parts, rx_hbm, rs_hbm, cou_hbm, w_hbm, qmap_hbm, qslot_hbm, inb,
           rx, cou, qmap, qslot, srow, xrow, scol, xcol, wst, pt, ysend, y, rout, tout, tin, acc,
           lsem, ssem, rsem):
    width = srow.shape[1]
    nb = rx.shape[0]
    chunk = xrow.shape[2]
    kr = lax.axis_index("krow")
    tr = lax.axis_index("tri")
    px, pc = kr // CORES, kr % CORES
    pz, py = tr // SIDE, tr % SIDE

    def plane_at(b):
        return ((pz + b[1]) % SIDE) * SIDE + (py + b[0]) % SIDE

    def line_at(dx, dc):
        return ((px + dx) % SIDE) * CORES + (pc + dc) % CORES

    def block(index):
        return pl.ds(pl.multiple_of(index * nb, nb), nb)

    def row(k, slot):
        rows = pl.ds(slot * nb, nb)
        return srow.at[rows] if k == 0 else xrow.at[k - 1, rows]

    def col(k, o):
        return scol.at[block(o)] if k == 0 else xcol.at[k - 1, block(o)]

    line = [(dx, dc) for dx in range(SIDE) for dc in range(CORES) if (dx, dc) != (0, 0)]
    others = [(dy, dz) for dy in range(SIDE) for dz in range(SIDE) if (dy, dz) != (0, 0)]

    barrier = pltpu.get_barrier_semaphore()
    for b in others:
        pl.semaphore_signal(barrier, inc=1, device_id={"tri": plane_at(b)}, device_id_type=MESH)
    for dx, dc in line:
        pl.semaphore_signal(barrier, inc=1, device_id={"krow": line_at(dx, dc)}, device_id_type=MESH)

    loads = [
        pltpu.make_async_copy(src, dst, lsem.at[i])
        for i, (src, dst) in enumerate((
            (rx_hbm, rx), (cou_hbm, cou), (rs_hbm, srow.at[0:nb]), (rs_hbm, scol.at[block(kr)]),
            (w_hbm.at[block(kr)], wst.at[tr]), (qmap_hbm, qmap), (qslot_hbm, qslot),
        ))
    ]
    for load in loads:
        load.start()

    def scale(k):
        if not scaled:
            loads[0].wait()
            loads[1].wait()
        scaled.add(k)
        lanes = pl.ds((k - 1) * chunk, chunk)
        own = (rx[:, lanes].astype(jnp.float32) * jnp.sqrt(cou[lanes]).reshape(1, chunk)).astype(jnp.bfloat16)
        xrow[k - 1, 0:nb, :] = own
        xcol[k - 1, block(kr), :] = own

    pl.semaphore_wait(barrier, len(others) + len(line))

    copies = {}

    def send(name, src, dst, device):
        i = len(copies)
        copies[name] = pltpu.make_async_remote_copy(
            src_ref=src, dst_ref=dst, send_sem=ssem.at[i], recv_sem=rsem.at[i],
            device_id=device, device_id_type=MESH,
        )
        copies[name].start()

    scaled = set()

    def pass_on(name):
        kind = name[0]
        if kind in ("row", "col") and name[-1] not in scaled | {0}:
            scale(name[-1])
        if kind == "w":
            b, e = name[1], source[name]
            held = wst.at[plane_at(less(b, e))]
            own = w_hbm.at[block(kr)] if less(b, e) == (0, 0) else held
            send(name, own, held, {"tri": plane_at((-e[0], -e[1]))})
        elif kind == "row":
            b, k = name[1:]
            e = source[name]
            own = rs_hbm if k == 0 and less(b, e) == (0, 0) else row(k, ROWS.index(less(b, e)))
            send(name, own, row(k, ROWS.index(b)), {"tri": plane_at((-e[0], -e[1]))})
        elif kind == "col":
            dx, k = name[1:]
            send(name, col(k, kr) if k else rs_hbm, col(k, kr), {"krow": line_at(-dx, 0)})
        elif kind == "far":
            dx, k = name[1:]
            held = col(k, line_at(dx, 0)).at[pl.ds(0 if dx == 1 else nb // 2, nb // 2)]
            send(name, held, held, {"krow": line_at(-dx, 0)})
        elif kind == "sib":
            dx, k = name[1:]
            held = col(k, line_at(dx, 0))
            send(name, rs_hbm if (dx, k) == (0, 0) else held, held, {"krow": line_at(0, 1)})
        else:
            project()

    def project():
        for load in loads[2:]:
            load.wait()
        pt[...] = (
            lax.dot_general(
                wst[...].reshape(PLANE * nb, width), scol[...], (((1,), (1,)), ((), ())),
                preferred_element_type=jnp.float32,
            ) * -0.5
        ).astype(jnp.bfloat16).reshape(pt.shape)
        low = lax.broadcasted_iota(jnp.int32, (nb, 2 * nb), 1) < nb
        for dx, dc in line + [(0, 0)]:
            o = line_at(dx, dc)
            for q in range(GROUPS // 2):
                lanes = pl.ds(q * 2 * nb, 2 * nb)
                first = pt[qslot[qmap[o, 2 * q]], :, lanes]
                second = pt[qslot[qmap[o, 2 * q + 1]], :, lanes]
                ysend[o, :, lanes] = jnp.where(low, first, second)
            if (dx, dc) == (0, 0):
                y[block(kr), :] = ysend[kr]
            else:
                send(("y", dx, dc), ysend.at[o], y.at[block(kr)], {"krow": o})

    def rows_of(group):
        return slice(group * 2 * nb, (group + 1) * 2 * nb)

    def work(group, k):
        rows = rows_of(group)
        if k == 0:
            part = jnp.dot(srow[rows, :], y[...], preferred_element_type=jnp.float32)
        else:
            part = lax.dot_general(
                xrow[k - 1, rows, :], xcol[k - 1], (((1,), (1,)), ((), ())), preferred_element_type=jnp.float32
            )
        total = part if not done[group] else acc[rows, :] + part
        done[group] += 1
        if done[group] <= parts:
            acc[rows, :] = total
        else:
            finish(group, total)

    def finish(group, total):
        rows = rows_of(group)
        total = total * 2.0
        if 2 * group in FLIP:
            i = FLIP.index(2 * group)
            tout[i] = total.T.astype(jnp.bfloat16)
            for dx, dc in line:
                o = line_at(dx, dc)
                send(("flip", i, dx, dc), tout.at[i, block(o)], tin.at[i, block(kr)], {"krow": o})
            tin[i, block(kr), :] = tout[i, block(kr), :]
        rout[rows, :] = total.astype(jnp.bfloat16)
        for slot in (2 * group, 2 * group + 1):
            b = ROWS[slot]
            if slot in OUT:
                send(("out", b), rout.at[pl.ds(slot * nb, nb)], inb.at[tr], {"tri": plane_at(b)})
        sent.append(group)

    def gather(group):
        if group == 0:
            inb[tr] = rout[0:nb, :]
        if 2 * group in FLIP:
            i = FLIP.index(2 * group)
            for dx, dc in line:
                copies["flip", i, dx, dc].wait_recv()
            for q in range(GROUPS // 2):
                got = mix(tin[i, 2 * q * nb : (2 * q + 1) * nb, :], tin[i, (2 * q + 1) * nb : (2 * q + 2) * nb, :])
                for half in range(2):
                    if 2 * group + half:
                        inb[plane_at(ROWS[2 * group + half]), :, q * 2 * nb : (q + 1) * 2 * nb] = got[half].astype(inb.dtype)

    sent = []
    cost = [2 * 2 * nb * (chunk if k else width) / RATE for k in range(parts + 1)]
    links = transfers(parts, cost)
    steps = schedule(links)
    source = {name: link for link, order in links.items() for name, _, _ in order}

    def names(kind, k=None, blocks=None):
        return [n for n in source if n[0] == kind and k in (None, n[-1]) and (blocks is None or n[1] in blocks)]

    def columns(k):
        return names("col", k) + names("far", k) + names("sib", k)

    done = [0] * (len(ROWS) // 2)
    tasks = []
    for k in range(parts + 1):
        for group in range(len(ROWS) // 2):
            blocks = ROWS[2 * group : 2 * group + 2]
            need = names("row", k, blocks) + (columns(k) if k else names("y"))
            tasks.append((set(need), functools.partial(work, group, k)))

    seen = set()
    for _, start, name in steps:
        if start:
            pass_on(name)
            continue
        for copy in [copies["y", dx, dc] for dx, dc in line] if name == ("y",) else [copies[name]]:
            copy.wait_recv()
        seen.add(name)
        for task in [t for t in tasks if seen >= t[0]]:
            task[1]()
            tasks.remove(task)

    while sent:
        gather(sent.pop(0))
    for slot in OUT:
        copies["out", ROWS[slot]].wait_recv()
    for copy in copies.values():
        copy.wait_send()


def mix(first, second):
    nb = first.shape[0]
    low = lax.broadcasted_iota(jnp.int32, first.shape, 1) < nb
    first, second = first.astype(jnp.float32), second.astype(jnp.float32)
    return jnp.where(low, first, pltpu.roll(second, nb, 1)), jnp.where(low, pltpu.roll(first, nb, 1), second)


def widen(src, dst, held, wide, sem_in, sem_out):
    pieces, plane, nb, tile = held.shape
    span = plane * nb
    reads = [
        pltpu.make_async_copy(src.at[:, :, pl.ds(q * tile, tile)], held.at[q], sem_in.at[q]) for q in range(pieces)
    ]
    writes = [
        pltpu.make_async_copy(wide.at[q], dst.at[:, pl.ds(q * 2 * span, 2 * span)], sem_out.at[q]) for q in range(pieces)
    ]
    for read in reads:
        read.start()
    for q in range(pieces):
        reads[q].wait()
        for m in range(plane // 2):
            for half, got in enumerate(mix(held[q, 2 * m], held[q, 2 * m + 1])):
                at = half * span + m * tile
                wide[q, :, at : at + tile] = got
        writes[q].start()
    for write in writes:
        write.wait()


def body(rho_x, rho_s, coulomb, screening, qmap, qslot):
    kpoints, npair, waves = rho_x.shape
    width = rho_s.shape[-1]
    nb = kpoints * npair
    parts = PARTS
    chunk = waves // parts
    cols = GROUPS * nb
    bf16, f32 = jnp.bfloat16, jnp.float32
    vmem = pl.BlockSpec(memory_space=pltpu.VMEM)
    hbm = pl.BlockSpec(memory_space=pltpu.HBM)
    ncopies = 15 + (9 + 4 + 4) * (parts + 1) + 7 + len(OUT) + 7 * len(FLIP)
    out = pl.pallas_call(
        functools.partial(kernel, parts),
        out_shape=jax.ShapeDtypeStruct((PLANE, nb, cols), bf16),
        in_specs=[hbm] * 6,
        out_specs=vmem,
        scratch_shapes=[
            pltpu.VMEM((nb, waves), bf16),
            pltpu.VMEM((waves,), f32),
            pltpu.SMEM(qmap.shape, jnp.int32),
            pltpu.SMEM(qslot.shape, jnp.int32),
            pltpu.VMEM((len(ROWS) * nb, width), bf16),
            pltpu.VMEM((parts, len(ROWS) * nb, chunk), bf16),
            pltpu.VMEM((cols, width), bf16),
            pltpu.VMEM((parts, cols, chunk), bf16),
            pltpu.VMEM((PLANE, nb, width), bf16),
            pltpu.VMEM((PLANE, nb, cols), bf16),
            pltpu.VMEM((GROUPS, nb, cols), bf16),
            pltpu.VMEM((width, cols), bf16),
            pltpu.VMEM((len(ROWS) * nb, cols), bf16),
            pltpu.VMEM((len(FLIP), cols, 2 * nb), bf16),
            pltpu.VMEM((len(FLIP), cols, 2 * nb), bf16),
            pltpu.VMEM((len(ROWS) * nb, cols), f32),
            pltpu.SemaphoreType.DMA((7,)),
            pltpu.SemaphoreType.DMA((ncopies,)),
            pltpu.SemaphoreType.DMA((ncopies,)),
        ],
        compiler_params=pltpu.CompilerParams(
            collective_id=0, has_side_effects=True, vmem_limit_bytes=62 * 2**20
        ),
        name="kernel_rows",
    )(
        rho_x.reshape(nb, waves),
        rho_s.reshape(nb, width),
        coulomb,
        screening.reshape(width, width),
        qmap,
        qslot,
    )
    pieces = GROUPS // 2
    out = pl.pallas_call(
        widen,
        out_shape=jax.ShapeDtypeStruct((nb, PLANE * cols), f32),
        in_specs=[hbm],
        out_specs=hbm,
        scratch_shapes=[
            pltpu.VMEM((pieces, PLANE, nb, 2 * nb), bf16),
            pltpu.VMEM((pieces, nb, PLANE * cols // pieces), f32),
            pltpu.SemaphoreType.DMA((pieces,)),
            pltpu.SemaphoreType.DMA((pieces,)),
        ],
        compiler_params=pltpu.CompilerParams(vmem_limit_bytes=62 * 2**20),
        name="widen",
    )(out)
    return out.reshape(kpoints, npair, -1)


def solution(mesh):
    placed = (
        P(("krow", "tri"), None, None),
        P(("krow", "tri"), None, None),
        P(),
        P("tri", None, None),
        P(),
        P(),
    )
    return jax.shard_map(
        body, mesh=mesh, in_specs=placed, out_specs=P(("krow", "tri"), None, None), check_vma=False
    )
```
